512 devices in a mesh: theta: 32 (over x_lo, z, core), gz: 16 (over y, x_hi).
Axes of the slice: x: 4 (x_hi: 2, x_lo: 2; x = x_hi * 2 + x_lo), y: 8, z: 8, core: 2. Of those that a mesh axis runs over, the one named last changes fastest.
Arguments:
- velocity: float32 [3, 256, 256, 256], P(None, 'theta', 'gz'), may hold values from -6 to 6
- adjoint_seed: float32 [3, 256, 256, 256], P(None, 'theta', 'gz'), may hold values from -6 to 6
- rotor_offset: int32 [2], replicated, may hold values from 0 to 255
- design_mask: int32 [256, 256, 256], P('theta', 'gz'), may hold values 0 or 1
- interface_band_weight: bfloat16 [256, 8], replicated, may hold values from -0.375 to 0.375
Outputs:
- ending_velocity: float32 [3, 256, 256, 256], P(None, 'theta', 'gz')
- adjoint_field: float32 [3, 256, 256, 256], P(None, 'theta', 'gz')
The draws below stay inside these ranges and needn't reach their ends.
All inputs are finite; a program needn't handle non-finite values. No bound on the sum of `design_mask` on one device may be relied on, other than what follows from the above.
Results may differ from the reference program's by a relative error of at most 0.00076.
Values sent between devices are 32-bit elements; how exact they have to be, the bound alone decides.
No kernel may reach another device: no remote copies, remote signals or barrier semaphores. Data moves between devices by JAX's collectives and lax.ppermute only.
A program may use at most 64 MiB of HBM per device.

```python
import jax
import jax.numpy as jnp

NR = 256
RB = 128
BAND = 8
STEPS = 2
NT = 256
NZ = 256


def set_ends(array, key, low, top_value):
    extent = array.shape
    spot = [jax.random.randint(jax.random.fold_in(key, axis), (), 0, extent[axis]) for axis in range(len(extent))]
    array = array.at[tuple(spot)].set(low)
    longest = extent.index(max(extent))
    spot[longest] = (spot[longest] + 1) % extent[longest]
    return array.at[tuple(spot)].set(top_value)


def block_scale(rng, shape, shards, least, high):
    loudness = 1.0
    for axis_at, shards_of in shards:
        steps = jax.random.uniform(jax.random.fold_in(jax.random.fold_in(rng, 6), axis_at), (shards_of,), jnp.float32, least / len(shards), high / len(shards))
        loudness = loudness * jnp.repeat(jnp.exp(steps), shape[axis_at] // shards_of).reshape((-1,) + (1,) * (len(shape) - 1 - axis_at))
    return loudness


def normal_values(rng, dims, spread, most, split=(), dtype=jnp.bfloat16):
    entries = jax.random.normal(rng, dims, jnp.float32) * spread
    if len(split) > 0:
        entries = block_scale(rng, dims, split, -0.22, 0.18) * entries
    return jnp.clip(entries, min=-most, max=most).astype(dtype)


def setup_inputs(seed: int = 0) -> dict:
    splits = jax.random.split(jax.random.key(seed), 6)
    return {
        "velocity": normal_values(splits[0], (3, NT, NZ, NR), 1.0, 6.0, ((1, 32), (2, 16)), jnp.float32),
        "adjoint_seed": normal_values(splits[1], (3, NT, NZ, NR), 1.0, 6.0, ((1, 32), (2, 16)), jnp.float32),
        "rotor_offset": jax.random.randint(splits[2], (STEPS,), 0, NT).astype(jnp.int32),
        "design_mask": set_ends((jax.random.randint(splits[3], (NT, NZ, NR), 0, 2) < 1).astype(jnp.int32), jax.random.fold_in(splits[3], 1), 0, 1),
        "interface_band_weight": normal_values(splits[4], (NR, BAND), NR ** -0.5, 0.375),
    }


def rotate(x, shift):
    rotor = jnp.roll(x[..., :RB], shift, axis=1)
    return jnp.concatenate([rotor, x[..., RB:]], axis=3)


def neighbours(x):
    tp = jnp.roll(x, -1, axis=1)
    tm = jnp.roll(x, 1, axis=1)
    zpad = jnp.pad(x, ((0, 0), (0, 0), (1, 1), (0, 0)))
    rpad = jnp.pad(x, ((0, 0), (0, 0), (0, 0), (1, 1)))
    return tp, tm, zpad[:, :, 2:], zpad[:, :, :-2], rpad[..., 2:], rpad[..., :-2]


def reference(velocity, adjoint_seed, rotor_offset, design_mask, interface_band_weight):
    lower = RB - BAND // 2
    upper = RB + BAND // 2
    solid = design_mask.astype(jnp.float32)
    flow_field = velocity
    viscosity_values = []
    for step in range(STEPS):
        moved = rotate(flow_field, rotor_offset[step])
        flat = moved.astype(jnp.bfloat16).reshape(-1, NR)
        mix = jnp.dot(flat, interface_band_weight, preferred_element_type=jnp.float32)
        mixed = moved.at[..., lower:upper].add(mix.reshape(3, NT, NZ, BAND))
        tp, tm, zp, zm, rp, rm = neighbours(mixed)
        strain_rate = jnp.sum(((tp - tm) * 0.5) ** 2 + ((zp - zm) * 0.5) ** 2 + ((rp - rm) * 0.5) ** 2, axis=0)
        visc = 0.05 + 0.95 * (1.0 + 4.0 * strain_rate) ** (-0.25)
        viscosity_values.append(visc)
        laplace = tp + tm + zp + zm + rp + rm - 6.0 * mixed
        flow_field = mixed + 0.1 * visc * laplace - 0.5 * solid * mixed
    adjoint = adjoint_seed
    for step in range(STEPS - 1, -1, -1):
        scaled = viscosity_values[step] * adjoint
        tp, tm, zp, zm, rp, rm = neighbours(scaled)
        laplace = tp + tm + zp + zm + rp + rm - 6.0 * scaled
        after = adjoint + 0.1 * laplace - 0.5 * solid * adjoint
        band = after[..., lower:upper].astype(jnp.bfloat16).reshape(-1, BAND)
        back = jnp.dot(band, interface_band_weight.T, preferred_element_type=jnp.float32)
        after = after + back.reshape(3, NT, NZ, NR)
        adjoint = rotate(after, -rotor_offset[step])
    return flow_field, adjoint
```

```python
import jax
import jax.numpy as jnp
from jax import lax
from jax.sharding import PartitionSpec as P

NR = 256
RB = 128
BAND = 8
STEPS = 2


def shifted(x, axis, by):
    peers = lax.axis_size(axis)
    return lax.ppermute(x, axis, [(i, (i + by) % peers) for i in range(peers)])


def padded(block, sides, width, periodic):
    for axis, dim in sides:
        count = lax.axis_size(axis)
        forward = [(i, i + 1) for i in range(count - 1)]
        if periodic:
            forward.append((count - 1, 0))
        backward = [(target, source) for source, target in forward]
        low = lax.ppermute(
            lax.slice_in_dim(block, block.shape[dim] - width, None, axis=dim), axis, forward
        )
        high = lax.ppermute(lax.slice_in_dim(block, 0, width, axis=dim), axis, backward)
        block = jnp.concatenate([low, block, high], axis=dim)
    return block


def rotate(flow_field, shift):
    sector_count = lax.axis_size("theta")
    width = flow_field.shape[1]
    shift = jnp.mod(shift, width * sector_count)
    blocks = shift // width
    remain = shift % width
    rotor = flow_field[..., :RB]

    def moved_by(count):
        return lambda x: (shifted(x, "theta", count + 1), shifted(x, "theta", count))

    before, here = lax.switch(blocks, [moved_by(b) for b in range(sector_count)], rotor)
    combined_parts = jnp.concatenate([before, here], axis=1)
    rotor = lax.dynamic_slice_in_dim(combined_parts, width - remain, width, axis=1)
    return jnp.concatenate([rotor, flow_field[..., RB:]], axis=3)


def neighbours(flow_field):
    beside_all = padded(flow_field, (("theta", 1),), 1, True)
    sliced_layers = padded(flow_field, (("gz", 2),), 1, False)
    radial = jnp.pad(flow_field, ((0, 0), (0, 0), (0, 0), (1, 1)))
    return (
        beside_all[:, 2:],
        beside_all[:, :-2],
        sliced_layers[:, :, 2:],
        sliced_layers[:, :, :-2],
        radial[..., 2:],
        radial[..., :-2],
    )


def body(velocity, adjoint_seed, rotor_offset, design_mask, interface_band_weight):
    lower = RB - BAND // 2
    upper = RB + BAND // 2
    shape = velocity.shape
    solid = design_mask.astype(jnp.float32)
    spread = jnp.pad(interface_band_weight, ((0, 0), (lower, NR - upper)))
    flow_field = velocity
    viscosity_values = []
    for step in range(STEPS):
        moved = rotate(flow_field, rotor_offset[step])
        flat = moved.astype(jnp.bfloat16).reshape(-1, NR)
        mix = jnp.dot(flat, spread, preferred_element_type=jnp.float32)
        mixed = moved + mix.reshape(shape)
        tp, tm, zp, zm, rp, rm = neighbours(mixed)
        strain_rate = jnp.sum(
            ((tp - tm) * 0.5) ** 2 + ((zp - zm) * 0.5) ** 2 + ((rp - rm) * 0.5) ** 2, axis=0
        )
        visc = 0.05 + 0.95 * (1.0 + 4.0 * strain_rate) ** (-0.25)
        viscosity_values.append(visc)
        laplace = tp + tm + zp + zm + rp + rm - 6.0 * mixed
        flow_field = mixed + 0.1 * visc * laplace - 0.5 * solid * mixed
    adjoint = adjoint_seed
    for step in range(STEPS - 1, -1, -1):
        scaled = viscosity_values[step] * adjoint
        tp, tm, zp, zm, rp, rm = neighbours(scaled)
        laplace = tp + tm + zp + zm + rp + rm - 6.0 * scaled
        after = adjoint + 0.1 * laplace - 0.5 * solid * adjoint
        band = after[..., lower:upper].astype(jnp.bfloat16).reshape(-1, BAND)
        back = jnp.dot(band, interface_band_weight.T, preferred_element_type=jnp.float32)
        after = after + back.reshape(shape)
        adjoint = rotate(after, -rotor_offset[step])
    return (flow_field, adjoint)


def solution(mesh):
    return jax.shard_map(
        body,
        mesh=mesh,
        in_specs=(
            P(None, "theta", "gz", None),
            P(None, "theta", "gz", None),
            P(),
            P("theta", "gz", None),
            P(),
        ),
        out_specs=(P(None, "theta", "gz", None), P(None, "theta", "gz", None)),
        check_vma=False,
    )
```

```python
import jax
import jax.numpy as jnp
from jax import lax
from jax.sharding import PartitionSpec as P

NR = 256
RB = 128
BAND = 8
STEPS = 2
LOWER = RB - BAND // 2
UPPER = RB + BAND // 2
ZH = 4


def shifted(x, axis, by):
    peers = lax.axis_size(axis)
    return lax.ppermute(x, axis, [(i, (i + by) % peers) for i in range(peers)])


def stepped(x, axis, by):
    peers = lax.axis_size(axis)
    return lax.ppermute(x, axis, [(i, i + by) for i in range(peers) if 0 <= i + by < peers])


def nearest(shift, width):
    half = width // 2
    return (shift + half) // width, (shift + half) % width - half


def to_block(rotor, blocks):
    peers = lax.axis_size("theta")
    moves = [lambda x, b=b: shifted(x, "theta", b) for b in range(peers)]
    return lax.switch(jnp.mod(blocks, peers), moves, rotor)


def exact(rotor, shift):
    peers = lax.axis_size("theta")
    width = rotor.shape[1]

    def move(total):
        blocks, rest = divmod(total, width)

        def run(x):
            here = shifted(x[:, : width - rest], "theta", blocks)
            if rest == 0:
                return here
            before = shifted(x[:, width - rest :], "theta", blocks + 1)
            return jnp.concatenate([before, here], axis=1)

        return run

    return lax.switch(jnp.mod(shift, width * peers), [move(s) for s in range(width * peers)], rotor)


def widened(rotor, stator, remain, h, extra=None):
    width = rotor.shape[1]
    reach = width // 2 + h
    up = [rotor[:, width - reach :], stator[:, width - h :]]
    down = [rotor[:, :reach], stator[:, :h]]
    if extra is not None:
        up += [extra[:, -1:, :, :RB], extra[:, -1:, :, RB:]]
        down += [extra[:, :1, :, :RB], extra[:, :1, :, RB:]]
    low = shifted(jnp.concatenate(up, axis=1), "theta", 1)
    high = shifted(jnp.concatenate(down, axis=1), "theta", -1)
    rotors = jnp.concatenate([low[:, :reach], rotor, high[:, :reach]], axis=1)
    aligned = lax.dynamic_slice_in_dim(rotors, reach - h - remain, width + 2 * h, axis=1)
    stators = jnp.concatenate([low[:, reach : reach + h], stator, high[:, reach : reach + h]], axis=1)
    whole = jnp.concatenate([aligned, stators], axis=3)
    if extra is None:
        return whole
    before = jnp.concatenate([low[:, reach + h : reach + h + 1], low[:, reach + h + 1 :]], axis=3)
    after = jnp.concatenate([high[:, reach + h : reach + h + 1], high[:, reach + h + 1 :]], axis=3)
    return whole, jnp.concatenate([before, extra, after], axis=1)


def beside(x):
    mid = x[:, 1:-1]
    zpad = jnp.pad(mid, ((0, 0), (0, 0), (1, 1), (0, 0)))
    rpad = jnp.pad(mid, ((0, 0), (0, 0), (0, 0), (1, 1)))
    return mid, x[:, 2:], x[:, :-2], zpad[:, :, 2:], zpad[:, :, :-2], rpad[..., 2:], rpad[..., :-2]


def viscosity(w):
    _, tp, tm, zp, zm, rp, rm = beside(w)
    strain_rate = jnp.sum(
        ((tp - tm) * 0.5) ** 2 + ((zp - zm) * 0.5) ** 2 + ((rp - rm) * 0.5) ** 2, axis=0
    )
    return 0.05 + 0.95 * (1.0 + 4.0 * strain_rate) ** (-0.25)


def laplace(x):
    mid, tp, tm, zp, zm, rp, rm = beside(x)
    return tp + tm + zp + zm + rp + rm - 6.0 * mid


def mixed(v, spread):
    flat = v.astype(jnp.bfloat16).reshape(-1, NR)
    return v + jnp.dot(flat, spread, preferred_element_type=jnp.float32).reshape(v.shape)


def coupled(a, weight):
    band = a[..., LOWER:UPPER].astype(jnp.bfloat16).reshape(-1, BAND)
    return a + jnp.dot(band, weight.T, preferred_element_type=jnp.float32).reshape(a.shape)


def axial_halo(field, seed, solid):
    nz = field.shape[2]

    def packed(cut):
        layers = jnp.moveaxis(cut(solid, 3, 1), 1, 0)[:, :, None]
        return jnp.concatenate(
            [cut(field, ZH, 2), cut(seed, 2, 2), layers, jnp.zeros_like(layers)], axis=2
        )

    low = stepped(packed(lambda x, n, d: lax.slice_in_dim(x, nz - n, nz, axis=d)), "gz", 1)
    high = stepped(packed(lambda x, n, d: lax.slice_in_dim(x, 0, n, axis=d)), "gz", -1)

    def layers_of(x):
        return jnp.moveaxis(x[:, :, ZH + 2], 0, 1)

    none = jnp.zeros_like(seed[:, :, :2])
    blank = jnp.zeros_like(solid[:, :1])
    return (
        jnp.concatenate([low[:, :, :ZH], field, high[:, :, :ZH]], axis=2),
        jnp.concatenate([none, low[:, :, ZH : ZH + 2], seed, high[:, :, ZH : ZH + 2], none], axis=2),
        jnp.concatenate([blank, layers_of(low), solid, layers_of(high), blank], axis=1),
    )


def body(velocity, adjoint_seed, rotor_offset, design_mask, interface_band_weight):
    width, nz = velocity.shape[1], velocity.shape[2]
    solid = design_mask.astype(jnp.float32)
    spread = jnp.pad(interface_band_weight, ((0, 0), (LOWER, NR - UPPER)))
    blocks0, remain0 = nearest(rotor_offset[0], width)
    blocks1, remain1 = nearest(rotor_offset[1], width)
    back1, away1 = nearest(-rotor_offset[1], width)

    rotor = to_block(velocity[..., :RB], blocks0)
    field = jnp.concatenate([rotor, velocity[..., RB:]], axis=3)
    field, seed, solid = axial_halo(field, adjoint_seed, solid)
    layer = lax.axis_index("gz") * nz - ZH + lax.broadcasted_iota(jnp.int32, (nz + 2 * ZH, 1), 0)
    inside = ((layer >= 0) & (layer < nz * lax.axis_size("gz"))).astype(jnp.float32)

    moved, seed = widened(field[..., :RB], field[..., RB:], remain0, 2, seed)
    w = mixed(moved, spread)
    visc0 = viscosity(w)
    mid = w[:, 2:-2]
    u = inside * (mid + 0.1 * visc0[1:-1] * laplace(w[:, 1:-1]) - 0.5 * solid * mid)

    rotor = to_block(u[..., :RB], blocks1)
    w = mixed(widened(rotor, u[..., RB:], remain1, 2), spread)
    visc1 = viscosity(w)
    mid = w[:, 2:-2]
    ending = (mid + 0.1 * visc1[1:-1] * laplace(w[:, 1:-1]) - 0.5 * solid * mid)[:, :, ZH:-ZH]
    lam = seed[:, 1:-1]
    lam = inside * coupled(lam + 0.1 * laplace(visc1 * seed) - 0.5 * solid * lam, interface_band_weight)

    rotor = to_block(lam[..., :RB], back1)
    lam = widened(rotor, lam[..., RB:], away1, 1)
    scaled = laplace(visc0 * lam)[:, :, ZH:-ZH]
    lam = lam[:, 1:-1, ZH:-ZH]
    lam = coupled(lam + 0.1 * scaled - 0.5 * solid[:, ZH:-ZH] * lam, interface_band_weight)
    rotor = exact(lam[..., :RB], -rotor_offset[0])
    return ending, jnp.concatenate([rotor, lam[..., RB:]], axis=3)


def solution(mesh):
    return jax.shard_map(
        body,
        mesh=mesh,
        in_specs=(
            P(None, "theta", "gz", None),
            P(None, "theta", "gz", None),
            P(),
            P("theta", "gz", None),
            P(),
        ),
        out_specs=(P(None, "theta", "gz", None), P(None, "theta", "gz", None)),
        check_vma=False,
    )
```

```python
import jax
import jax.numpy as jnp
from jax import lax
from jax.sharding import PartitionSpec as P

NR = 256
RB = 128
BAND = 8
STEPS = 2
LOWER = RB - BAND // 2
UPPER = RB + BAND // 2
ZH = 4


def shifted(x, axis, by):
    peers = lax.axis_size(axis)
    return lax.ppermute(x, axis, [(i, (i + by) % peers) for i in range(peers)])


def stepped(x, axis, by):
    peers = lax.axis_size(axis)
    return lax.ppermute(x, axis, [(i, i + by) for i in range(peers) if 0 <= i + by < peers])


def nearest(shift, width):
    half = width // 2
    return (shift + half) // width, (shift + half) % width - half


def to_block(rotor, blocks):
    peers = lax.axis_size("theta")
    moves = [lambda x, b=b: shifted(x, "theta", b) for b in range(peers)]
    return lax.switch(jnp.mod(blocks, peers), moves, rotor)


def exact(rotor, shift):
    peers = lax.axis_size("theta")
    width = rotor.shape[1]
    group = width // 2
    shift = jnp.mod(shift, width * peers)

    def move(total):
        blocks, rest = divmod(total * group, width)

        def run(x):
            here = shifted(x[:, : width - rest], "theta", blocks)
            before = shifted(x[:, width - rest - group + 1 :], "theta", blocks + 1)
            return jnp.concatenate([before, here], axis=1)

        return run

    rows = lax.switch(shift // group, [move(i) for i in range(peers * width // group)], rotor)
    return lax.dynamic_slice_in_dim(rows, group - 1 - shift % group, width, axis=1)


def widened(rotor, stator, remain, h, extra=None):
    width = rotor.shape[1]
    reach = width // 2 + h
    up = [rotor[:, width - reach :], stator[:, width - h :]]
    down = [rotor[:, :reach], stator[:, :h]]
    if extra is not None:
        up += [extra[:, -1:, :, :RB], extra[:, -1:, :, RB:]]
        down += [extra[:, :1, :, :RB], extra[:, :1, :, RB:]]
    low = shifted(jnp.concatenate(up, axis=1), "theta", 1)
    high = shifted(jnp.concatenate(down, axis=1), "theta", -1)
    rotors = jnp.concatenate([low[:, :reach], rotor, high[:, :reach]], axis=1)
    aligned = lax.dynamic_slice_in_dim(rotors, reach - h - remain, width + 2 * h, axis=1)
    stators = jnp.concatenate([low[:, reach : reach + h], stator, high[:, reach : reach + h]], axis=1)
    whole = jnp.concatenate([aligned, stators], axis=3)
    if extra is None:
        return whole
    before = jnp.concatenate([low[:, reach + h : reach + h + 1], low[:, reach + h + 1 :]], axis=3)
    after = jnp.concatenate([high[:, reach + h : reach + h + 1], high[:, reach + h + 1 :]], axis=3)
    return whole, jnp.concatenate([before, extra, after], axis=1)


def beside(x):
    mid = x[:, 1:-1]
    zpad = jnp.pad(mid, ((0, 0), (0, 0), (1, 1), (0, 0)))
    rpad = jnp.pad(mid, ((0, 0), (0, 0), (0, 0), (1, 1)))
    return mid, x[:, 2:], x[:, :-2], zpad[:, :, 2:], zpad[:, :, :-2], rpad[..., 2:], rpad[..., :-2]


def viscosity(w):
    _, tp, tm, zp, zm, rp, rm = beside(w)
    strain_rate = jnp.sum(
        ((tp - tm) * 0.5) ** 2 + ((zp - zm) * 0.5) ** 2 + ((rp - rm) * 0.5) ** 2, axis=0
    )
    return 0.05 + 0.95 * (1.0 + 4.0 * strain_rate) ** (-0.25)


def laplace(x):
    mid, tp, tm, zp, zm, rp, rm = beside(x)
    return tp + tm + zp + zm + rp + rm - 6.0 * mid


def mixed(v, spread):
    flat = v.astype(jnp.bfloat16).reshape(-1, NR)
    return v + jnp.dot(flat, spread, preferred_element_type=jnp.float32).reshape(v.shape)


def coupled(a, weight):
    band = a[..., LOWER:UPPER].astype(jnp.bfloat16).reshape(-1, BAND)
    return a + jnp.dot(band, weight.T, preferred_element_type=jnp.float32).reshape(a.shape)


def axial_halo(field, seed, solid):
    nz = field.shape[2]

    def packed(cut):
        layers = jnp.moveaxis(cut(solid, 3, 1), 1, 0)[:, :, None]
        return jnp.concatenate(
            [cut(field, ZH, 2), cut(seed, 2, 2), layers, jnp.zeros_like(layers)], axis=2
        )

    low = stepped(packed(lambda x, n, d: lax.slice_in_dim(x, nz - n, nz, axis=d)), "gz", 1)
    high = stepped(packed(lambda x, n, d: lax.slice_in_dim(x, 0, n, axis=d)), "gz", -1)

    def layers_of(x):
        return jnp.moveaxis(x[:, :, ZH + 2], 0, 1)

    none = jnp.zeros_like(seed[:, :, :2])
    blank = jnp.zeros_like(solid[:, :1])
    return (
        jnp.concatenate([low[:, :, :ZH], field, high[:, :, :ZH]], axis=2),
        jnp.concatenate([none, low[:, :, ZH : ZH + 2], seed, high[:, :, ZH : ZH + 2], none], axis=2),
        jnp.concatenate([blank, layers_of(low), solid, layers_of(high), blank], axis=1),
    )


def body(velocity, adjoint_seed, rotor_offset, design_mask, interface_band_weight):
    width, nz = velocity.shape[1], velocity.shape[2]
    solid = design_mask.astype(jnp.float32)
    spread = jnp.pad(interface_band_weight, ((0, 0), (LOWER, NR - UPPER)))
    blocks0, remain0 = nearest(rotor_offset[0], width)
    blocks1, remain1 = nearest(rotor_offset[1], width)
    back1, away1 = nearest(-rotor_offset[1], width)

    rotor = to_block(velocity[..., :RB], blocks0)
    field = jnp.concatenate([rotor, velocity[..., RB:]], axis=3)
    field, seed, solid = axial_halo(field, adjoint_seed, solid)
    layer = lax.axis_index("gz") * nz - ZH + lax.broadcasted_iota(jnp.int32, (nz + 2 * ZH, 1), 0)
    inside = ((layer >= 0) & (layer < nz * lax.axis_size("gz"))).astype(jnp.float32)

    moved, seed = widened(field[..., :RB], field[..., RB:], remain0, 2, seed)
    w = mixed(moved, spread)
    visc0 = viscosity(w)
    mid = w[:, 2:-2]
    u = inside * (mid + 0.1 * visc0[1:-1] * laplace(w[:, 1:-1]) - 0.5 * solid * mid)

    rotor = to_block(u[..., :RB], blocks1)
    w = mixed(widened(rotor, u[..., RB:], remain1, 2), spread)
    visc1 = viscosity(w)
    mid = w[:, 2:-2]
    ending = (mid + 0.1 * visc1[1:-1] * laplace(w[:, 1:-1]) - 0.5 * solid * mid)[:, :, ZH:-ZH]
    lam = seed[:, 1:-1]
    lam = inside * coupled(lam + 0.1 * laplace(visc1 * seed) - 0.5 * solid * lam, interface_band_weight)

    rotor = to_block(lam[..., :RB], back1)
    lam = widened(rotor, lam[..., RB:], away1, 1)
    scaled = laplace(visc0 * lam)[:, :, ZH:-ZH]
    lam = lam[:, 1:-1, ZH:-ZH]
    lam = coupled(lam + 0.1 * scaled - 0.5 * solid[:, ZH:-ZH] * lam, interface_band_weight)
    rotor = exact(lam[..., :RB], -rotor_offset[0])
    return ending, jnp.concatenate([rotor, lam[..., RB:]], axis=3)


def solution(mesh):
    return jax.shard_map(
        body,
        mesh=mesh,
        in_specs=(
            P(None, "theta", "gz", None),
            P(None, "theta", "gz", None),
            P(),
            P("theta", "gz", None),
            P(),
        ),
        out_specs=(P(None, "theta", "gz", None), P(None, "theta", "gz", None)),
        check_vma=False,
    )
```

```python
import jax
import jax.numpy as jnp
from jax import lax
from jax.sharding import PartitionSpec as P

NR = 256
RB = 128
BAND = 8
STEPS = 2
LOWER = RB - BAND // 2
UPPER = RB + BAND // 2
ZH = 4


def shifted(x, axis, by):
    peers = lax.axis_size(axis)
    return lax.ppermute(x, axis, [(i, (i + by) % peers) for i in range(peers)])


def swapped(up, down, axis, wraps):
    peers = lax.axis_size(axis)
    even = lax.axis_index(axis) % 2 == 0
    within = [(i, i ^ 1) for i in range(peers)]
    across = [(i, i + 1 if i % 2 else i - 1) for i in range(peers)]
    if wraps:
        across = [(i, j % peers) for i, j in across]
    else:
        across = [(i, j) for i, j in across if 0 <= j < peers]
    inner, outer = jnp.where(even, up, down), jnp.where(even, down, up)
    if wraps:
        inner = lax.ppermute(inner, axis, within)
        outer = lax.ppermute(outer, axis, across)
    else:
        outer = lax.ppermute(outer, axis, across)
        inner = lax.ppermute(inner, axis, within)
    return jnp.where(even, outer, inner), jnp.where(even, inner, outer)


def nearest(shift, width):
    half = width // 2
    return (shift + half) // width, (shift + half) % width - half


def to_block(rotor, blocks):
    peers = lax.axis_size("theta")
    moves = [lambda x, b=b: shifted(x, "theta", b) for b in range(peers)]
    return lax.switch(jnp.mod(blocks, peers), moves, rotor)


def exact(rotor, shift):
    peers = lax.axis_size("theta")
    width = rotor.shape[1]
    group = width // 2
    shift = jnp.mod(shift, width * peers)

    def move(total):
        blocks, rest = divmod(total * group, width)

        def run(x):
            here = shifted(x[:, : width - rest], "theta", blocks)
            before = shifted(x[:, width - rest - group + 1 :], "theta", blocks + 1)
            return jnp.concatenate([before, here], axis=1)

        return run

    rows = lax.switch(shift // group, [move(i) for i in range(peers * width // group)], rotor)
    return lax.dynamic_slice_in_dim(rows, group - 1 - shift % group, width, axis=1)


def widened(rotor, stator, remain, h, extra=None):
    width = rotor.shape[1]
    reach = width // 2 + h
    up = [rotor[:, width - reach :], stator[:, width - h :]]
    down = [rotor[:, :reach], stator[:, :h]]
    if extra is not None:
        up += [extra[:, -1:, :, :RB], extra[:, -1:, :, RB:]]
        down += [extra[:, :1, :, :RB], extra[:, :1, :, RB:]]
    low, high = swapped(jnp.concatenate(up, axis=1), jnp.concatenate(down, axis=1), "theta", True)
    rotors = jnp.concatenate([low[:, :reach], rotor, high[:, :reach]], axis=1)
    aligned = lax.dynamic_slice_in_dim(rotors, reach - h - remain, width + 2 * h, axis=1)
    stators = jnp.concatenate([low[:, reach : reach + h], stator, high[:, reach : reach + h]], axis=1)
    whole = jnp.concatenate([aligned, stators], axis=3)
    if extra is None:
        return whole
    before = jnp.concatenate([low[:, reach + h : reach + h + 1], low[:, reach + h + 1 :]], axis=3)
    after = jnp.concatenate([high[:, reach + h : reach + h + 1], high[:, reach + h + 1 :]], axis=3)
    return whole, jnp.concatenate([before, extra, after], axis=1)


def beside(x):
    mid = x[:, 1:-1]
    zpad = jnp.pad(mid, ((0, 0), (0, 0), (1, 1), (0, 0)))
    rpad = jnp.pad(mid, ((0, 0), (0, 0), (0, 0), (1, 1)))
    return mid, x[:, 2:], x[:, :-2], zpad[:, :, 2:], zpad[:, :, :-2], rpad[..., 2:], rpad[..., :-2]


def viscosity(w):
    _, tp, tm, zp, zm, rp, rm = beside(w)
    strain_rate = jnp.sum(
        ((tp - tm) * 0.5) ** 2 + ((zp - zm) * 0.5) ** 2 + ((rp - rm) * 0.5) ** 2, axis=0
    )
    return 0.05 + 0.95 * (1.0 + 4.0 * strain_rate) ** (-0.25)


def laplace(x):
    mid, tp, tm, zp, zm, rp, rm = beside(x)
    return tp + tm + zp + zm + rp + rm - 6.0 * mid


def mixed(v, spread):
    flat = v.astype(jnp.bfloat16).reshape(-1, NR)
    return v + jnp.dot(flat, spread, preferred_element_type=jnp.float32).reshape(v.shape)


def coupled(a, weight):
    band = a[..., LOWER:UPPER].astype(jnp.bfloat16).reshape(-1, BAND)
    return a + jnp.dot(band, weight.T, preferred_element_type=jnp.float32).reshape(a.shape)


def axial_halo(field, seed, solid):
    nz = field.shape[2]

    def packed(cut):
        layers = jnp.moveaxis(cut(solid, 3, 1), 1, 0)[:, :, None]
        return jnp.concatenate(
            [cut(field, ZH, 2), cut(seed, 2, 2), layers, jnp.zeros_like(layers)], axis=2
        )

    top = packed(lambda x, n, d: lax.slice_in_dim(x, nz - n, nz, axis=d))
    bottom = packed(lambda x, n, d: lax.slice_in_dim(x, 0, n, axis=d))
    low, high = swapped(top, bottom, "gz", False)

    def layers_of(x):
        return jnp.moveaxis(x[:, :, ZH + 2], 0, 1)

    none = jnp.zeros_like(seed[:, :, :2])
    blank = jnp.zeros_like(solid[:, :1])
    return (
        jnp.concatenate([low[:, :, :ZH], field, high[:, :, :ZH]], axis=2),
        jnp.concatenate([none, low[:, :, ZH : ZH + 2], seed, high[:, :, ZH : ZH + 2], none], axis=2),
        jnp.concatenate([blank, layers_of(low), solid, layers_of(high), blank], axis=1),
    )


def body(velocity, adjoint_seed, rotor_offset, design_mask, interface_band_weight):
    width, nz = velocity.shape[1], velocity.shape[2]
    solid = design_mask.astype(jnp.float32)
    spread = jnp.pad(interface_band_weight, ((0, 0), (LOWER, NR - UPPER)))
    blocks0, remain0 = nearest(rotor_offset[0], width)
    blocks1, remain1 = nearest(rotor_offset[1], width)
    back1, away1 = nearest(-rotor_offset[1], width)

    rotor = to_block(velocity[..., :RB], blocks0)
    field = jnp.concatenate([rotor, velocity[..., RB:]], axis=3)
    field, seed, solid = axial_halo(field, adjoint_seed, solid)
    layer = lax.axis_index("gz") * nz - ZH + lax.broadcasted_iota(jnp.int32, (nz + 2 * ZH, 1), 0)
    inside = ((layer >= 0) & (layer < nz * lax.axis_size("gz"))).astype(jnp.float32)

    moved, seed = widened(field[..., :RB], field[..., RB:], remain0, 2, seed)
    w = mixed(moved, spread)
    visc0 = viscosity(w)
    mid = w[:, 2:-2]
    u = inside * (mid + 0.1 * visc0[1:-1] * laplace(w[:, 1:-1]) - 0.5 * solid * mid)

    rotor = to_block(u[..., :RB], blocks1)
    w = mixed(widened(rotor, u[..., RB:], remain1, 2), spread)
    visc1 = viscosity(w)
    mid = w[:, 2:-2]
    ending = (mid + 0.1 * visc1[1:-1] * laplace(w[:, 1:-1]) - 0.5 * solid * mid)[:, :, ZH:-ZH]
    lam = seed[:, 1:-1]
    lam = inside * coupled(lam + 0.1 * laplace(visc1 * seed) - 0.5 * solid * lam, interface_band_weight)

    rotor = to_block(lam[..., :RB], back1)
    lam = widened(rotor, lam[..., RB:], away1, 1)
    scaled = laplace(visc0 * lam)[:, :, ZH:-ZH]
    lam = lam[:, 1:-1, ZH:-ZH]
    lam = coupled(lam + 0.1 * scaled - 0.5 * solid[:, ZH:-ZH] * lam, interface_band_weight)
    rotor = exact(lam[..., :RB], -rotor_offset[0])
    return ending, jnp.concatenate([rotor, lam[..., RB:]], axis=3)


def solution(mesh):
    return jax.shard_map(
        body,
        mesh=mesh,
        in_specs=(
            P(None, "theta", "gz", None),
            P(None, "theta", "gz", None),
            P(),
            P("theta", "gz", None),
            P(),
        ),
        out_specs=(P(None, "theta", "gz", None), P(None, "theta", "gz", None)),
        check_vma=False,
    )
```

```python
import jax
import jax.numpy as jnp
from jax import lax
from jax.experimental import pallas as pl
from jax.experimental.pallas import tpu as pltpu
from jax.sharding import PartitionSpec as P

NR = 256
RB = 128
BAND = 8
STEPS = 2
LOWER = RB - BAND // 2
UPPER = RB + BAND // 2
ZH = 4


def is_even(axis):
    return 1 - lax.rem(lax.axis_index(axis), 2)


def left_over(shift, width):
    half = width // 2
    return ((shift + half) & (width - 1)) - half


def call(kernel, outs, offsets, *arrays, scratch=()):
    whole = pl.BlockSpec(memory_space=pltpu.VMEM)
    return pl.pallas_call(
        kernel,
        out_shape=[jax.ShapeDtypeStruct(shape, jnp.float32) for shape in outs],
        in_specs=[pl.BlockSpec(memory_space=pltpu.SMEM)] + [whole] * len(arrays),
        out_specs=[whole] * len(outs),
        scratch_shapes=[pltpu.VMEM(shape, jnp.float32) for shape in scratch],
        compiler_params=pltpu.CompilerParams(vmem_limit_bytes=24 << 20),
    )(offsets, *arrays)


def shifted(x, axis, by):
    peers = lax.axis_size(axis)
    return lax.ppermute(x, axis, [(i, (i + by) % peers) for i in range(peers)])


def nearest(shift, width):
    return (shift + width // 2) // width


def to_block(rotor, blocks):
    peers = lax.axis_size("theta")
    moves = [lambda x, b=b: shifted(x, "theta", b) for b in range(peers)]
    return lax.switch(jnp.mod(blocks, peers), moves, rotor)


def exact(rotor, shift):
    peers = lax.axis_size("theta")
    width = rotor.shape[1]
    group = width // 2
    shift = jnp.mod(shift, width * peers)

    def move(total):
        blocks, rest = divmod(total * group, width)

        def run(x):
            here = shifted(x[:, : width - rest], "theta", blocks)
            before = shifted(x[:, width - rest - group + 1 :], "theta", blocks + 1)
            return jnp.concatenate([before, here], axis=1)

        return run

    return lax.switch(shift // group, [move(i) for i in range(peers * width // group)], rotor)


def swapped(inner, outer, axis, wraps):
    peers = lax.axis_size(axis)
    within = [(i, i ^ 1) for i in range(peers)]
    across = [(i, i + 1 if i % 2 else i - 1) for i in range(peers)]
    if wraps:
        outer = lax.ppermute(outer, axis, [(i, j % peers) for i, j in across])
        return lax.ppermute(inner, axis, within), outer
    inner = lax.ppermute(inner, axis, within)
    return inner, lax.ppermute(outer, axis, [(i, j) for i, j in across if 0 <= j < peers])


def pack_layers(offsets, rotor, velocity, seed_in, mask_in, inner, outer, stator, seed, mask, done):
    copies = [
        pltpu.make_async_copy(velocity.at[:, :, :, pl.ds(RB, RB)], stator, done.at[0]),
        pltpu.make_async_copy(seed_in, seed, done.at[1]),
        pltpu.make_async_copy(mask_in, mask, done.at[2]),
    ]
    for copy in copies:
        copy.start()
    for copy in copies:
        copy.wait()
    even = is_even("gz") == 1
    nz = rotor.shape[2]
    for c in range(3):
        for row in range(rotor.shape[1]):
            ends = []
            for z0, z1, z2 in ((nz - ZH, nz - 2, nz - 3 + c), (0, 0, c)):
                solid = mask[row, z2 : z2 + 1, :].astype(jnp.float32)
                blank = jnp.zeros((1, RB), jnp.float32)
                left = [rotor[c, row, z0 : z0 + ZH, :], seed[c, row, z1 : z1 + 2, :RB], solid[:, :RB], blank]
                right = [stator[c, row, z0 : z0 + ZH, :], seed[c, row, z1 : z1 + 2, RB:], solid[:, RB:], blank]
                ends.append([jnp.concatenate(left, axis=0), jnp.concatenate(right, axis=0)])
            top, bottom = ends
            for half in range(2):
                lanes = slice(half * RB, half * RB + RB)
                inner[c, row, :, lanes] = jnp.where(even, top[half], bottom[half])
                outer[c, row, :, lanes] = jnp.where(even, bottom[half], top[half])


def send_rows(h, rotor, stator, extra, inner, outer):
    width = rotor.shape[1]
    reach = width // 2 + h
    even = is_even("theta")
    for target, last in ((inner, even), (outer, 1 - even)):
        target[:, :reach] = rotor[:, pl.ds(last * (width - reach), reach)]
        target[:, reach : reach + h] = stator[:, pl.ds(last * (width - h), h)]
        if extra is not None:
            edge = extra[:, pl.ds(last * (width - 1), 1)]
            target[:, reach + h : reach + h + 1] = edge[..., :RB]
            target[:, reach + h + 1 :] = edge[..., RB:]


def unpack_layers(
    offsets, inner, outer, rotor, stator, seed, mask,
    rotor_out, stator_out, seed_out, solid_out, rows_out, rows_in,
):
    even = is_even("gz") == 1
    nz = rotor.shape[2]
    none = jnp.zeros((2, NR), jnp.float32)
    blank = jnp.zeros((1, NR), jnp.float32)
    for row in range(rotor.shape[1]):
        solid_above, solid_below = [], []
        for c in range(3):
            one, two = inner[c, row], outer[c, row]
            above, below = jnp.where(even, one, two), jnp.where(even, two, one)
            halo = jnp.concatenate([above[:ZH], below[:ZH]], axis=0)
            rotor_out[c, row, :nz, :] = rotor[c, row]
            rotor_out[c, row, nz:, :] = halo[:, :RB]
            stator_out[c, row, :nz, :] = stator[c, row]
            stator_out[c, row, nz:, :] = halo[:, RB:]
            seed_out[c, row, :nz, :] = seed[c, row]
            seed_out[c, row, nz:, :] = jnp.concatenate(
                [above[ZH : ZH + 2], none, none, below[ZH : ZH + 2]], axis=0
            )
            solid_above.append(above[ZH + 2 : ZH + 3])
            solid_below.append(below[ZH + 2 : ZH + 3])
        solid_out[row, :nz, :] = mask[row].astype(jnp.float32)
        solid_out[row, nz:, :] = jnp.concatenate(solid_above + [blank, blank] + solid_below, axis=0)
    send_rows(2, rotor_out, stator_out, seed_out, rows_in, rows_out)


def pack_rows(offsets, rotor, stator, outer, inner):
    send_rows(2, rotor, stator, None, inner, outer)


def pack_last_rows(offsets, packed, stator, outer, inner, rotor):
    _, width, layers, _ = rotor.shape
    nz = packed.shape[2]
    none = jnp.zeros((layers - nz - 2, RB), jnp.float32)
    for c in range(3):
        for row in range(width):
            rotor[c, row, :nz, :] = packed[c, row]
            beyond = packed[c, width, 2 * row : 2 * row + 2, :]
            rotor[c, row, nz:, :] = jnp.concatenate([beyond[:1], none, beyond[1:]], axis=0)
    send_rows(1, rotor, stator, None, inner, outer)


def gather(remain, h, inner, outer, rotor, stator, rotors, field):
    width = rotor.shape[1]
    reach = width // 2 + h
    even = is_even("theta")
    rotors[:, reach : reach + width] = rotor[...]
    rotors[:, pl.ds(even * (reach + width), reach)] = inner[:, :reach]
    rotors[:, pl.ds((1 - even) * (reach + width), reach)] = outer[:, :reach]
    field[..., :RB] = rotors[:, pl.ds(reach - h - remain, width + 2 * h)]
    field[:, h : h + width, :, RB:] = stator[...]
    field[:, pl.ds(even * (h + width), h), :, RB:] = inner[:, reach : reach + h]
    field[:, pl.ds((1 - even) * (h + width), h), :, RB:] = outer[:, reach : reach + h]


def multiply(rows, weight):
    flat = rows.astype(jnp.bfloat16).reshape(-1, NR)
    return rows + jnp.dot(flat, weight[...], preferred_element_type=jnp.float32).reshape(rows.shape)


def around(x, row):
    mid = x[row]
    layers = mid.shape[0]
    lane = lax.broadcasted_iota(jnp.int32, mid.shape, 1)
    rp = jnp.where(lane == NR - 1, 0.0, pltpu.roll(mid, NR - 1, 1))
    rm = jnp.where(lane == 0, 0.0, pltpu.roll(mid, 1, 1))
    return mid, x[row + 1], x[row - 1], pltpu.roll(mid, layers - 1, 0), pltpu.roll(mid, 1, 0), rp, rm


def laplace(mid, tp, tm, zp, zm, rp, rm):
    return tp + tm + zp + zm + rp + rm - 6.0 * mid


def viscosity(sides):
    total = 0.0
    for _, tp, tm, zp, zm, rp, rm in sides:
        total = total + (tp - tm) ** 2 + (zp - zm) ** 2 + (rp - rm) ** 2
    return 0.05 + 0.95 * lax.rsqrt(jnp.sqrt(1.0 + total))


def within_ends(layers):
    place = lax.broadcasted_iota(jnp.int32, (layers, NR), 0)
    nz = layers - 2 * ZH
    layer = lax.axis_index("gz") * nz + jnp.where(place >= layers - ZH, place - layers, place)
    return ((layer >= 0) & (layer < lax.axis_size("gz") * nz)).astype(jnp.float32)


def forward_first(offsets, outer, inner, rotor, stator, solid, weight, visc, u_rotor, u_stator, rotors, w):
    gather(left_over(offsets[0], rotor.shape[1]), 2, inner, outer, rotor, stator, rotors, w)
    for c in range(3):
        w[c] = multiply(w[c], weight)
    width, layers = rotor.shape[1:3]
    inside = within_ends(layers)
    for row in range(width + 2):
        sides = [around(w.at[c], row + 1) for c in range(3)]
        mu = viscosity(sides)
        visc[row] = mu
        if 1 <= row <= width:
            damp = 0.5 * solid[row - 1]
            for c in range(3):
                u = inside * (sides[c][0] + 0.1 * mu * laplace(*sides[c]) - damp * sides[c][0])
                u_rotor[c, row - 1] = u[:, :RB]
                u_stator[c, row - 1] = u[:, RB:]


def forward_last(
    offsets, outer, inner, rotor, stator, solid, weight, back_weight, seed, first_in, first_out,
    ending, lam_rotor, lam_stator, rotors, w, scaled, after,
):
    gather(left_over(offsets[1], rotor.shape[1]), 2, inner, outer, rotor, stator, rotors, w)
    for c in range(3):
        w[c] = multiply(w[c], weight)
    width, layers = rotor.shape[1:3]
    nz = layers - 2 * ZH
    even = is_even("theta") == 1
    inside = within_ends(layers)
    for row in range(width + 2):
        sides = [around(w.at[c], row + 1) for c in range(3)]
        mu = viscosity(sides)
        for c in range(3):
            if 1 <= row <= width:
                lam = seed[c, row - 1]
                scaled[c, row] = mu * lam
                mid = sides[c][0]
                u = mid + 0.1 * mu * laplace(*sides[c]) - 0.5 * solid[row - 1] * mid
                ending[c, row - 1] = u[:nz]
            else:
                one, two = (first_out, first_in) if row == 0 else (first_in, first_out)
                for half in range(2):
                    at = one.shape[1] - 2 + half
                    lam = jnp.where(even, one[c, at], two[c, at])
                    lanes = slice(half * RB, half * RB + RB)
                    scaled[c, row, :, lanes] = mu[:, lanes] * lam
    for c in range(3):
        for row in range(width):
            lam = seed[c, row]
            after[row] = lam + 0.1 * laplace(*around(scaled.at[c], row + 1)) - 0.5 * solid[row] * lam
        lam = inside * multiply(after[...], back_weight)
        lam_stator[c] = lam[..., RB:]
        lam_rotor[c, :width] = lam[:, :nz, :RB]
        for row in range(width):
            lam_rotor[c, width, 2 * row : 2 * row + 1, :] = lam[row, nz : nz + 1, :RB]
            lam_rotor[c, width, 2 * row + 1 : 2 * row + 2, :] = lam[row, layers - 1 :, :RB]


def adjoint_first(
    offsets, outer, inner, rotor, stator, solid, back_weight, visc, b_rotor, b_stator, rotors, lam, scaled, after
):
    gather(left_over(-offsets[1], rotor.shape[1]), 1, inner, outer, rotor, stator, rotors, lam)
    width, layers = rotor.shape[1:3]
    nz = layers - 2 * ZH
    for c in range(3):
        scaled[c] = visc[...] * lam[c]
        for row in range(width):
            mid = lam[c, row + 1]
            a = mid + 0.1 * laplace(*around(scaled.at[c], row + 1)) - 0.5 * solid[row] * mid
            after[row] = a[:nz]
        b = multiply(after[...], back_weight)
        b_rotor[c] = b[..., :RB]
        b_stator[c] = b[..., RB:]


def join(offsets, rows, stator, out):
    width = stator.shape[1]
    group = width // 2
    out[..., :RB] = rows[:, pl.ds(group - 1 - (-offsets[0] & (group - 1)), width)]
    out[..., RB:] = stator[...]


def load(offsets, rotor, velocity, seed, mask):
    _, width, nz, _ = velocity.shape
    edge = jax.ShapeDtypeStruct((3, width, 2 * ZH, NR), jnp.float32)
    whole = pl.BlockSpec(memory_space=pltpu.VMEM)
    far = pl.BlockSpec(memory_space=pl.ANY)
    return pl.pallas_call(
        pack_layers,
        out_shape=[
            edge,
            edge,
            jax.ShapeDtypeStruct((3, width, nz, RB), jnp.float32),
            jax.ShapeDtypeStruct(seed.shape, jnp.float32),
            jax.ShapeDtypeStruct(mask.shape, jnp.int32),
        ],
        in_specs=[pl.BlockSpec(memory_space=pltpu.SMEM), whole, far, far, far],
        out_specs=[whole] * 5,
        scratch_shapes=[pltpu.SemaphoreType.DMA((3,))],
        compiler_params=pltpu.CompilerParams(vmem_limit_bytes=24 << 20),
    )(offsets, rotor, velocity, seed, mask)


def body(velocity, adjoint_seed, rotor_offset, design_mask, interface_band_weight):
    _, width, nz, _ = velocity.shape
    zs = nz + 2 * ZH
    spread = jnp.pad(interface_band_weight, ((0, 0), (LOWER, NR - UPPER)))
    back_weight = jnp.pad(interface_band_weight.T, ((LOWER, NR - UPPER), (0, 0)))
    blocks0 = nearest(rotor_offset[0], width)
    blocks1 = nearest(rotor_offset[1], width)
    back1 = nearest(-rotor_offset[1], width)
    group = width // 2
    block = (3, width, zs, RB)

    def ext(rows):
        return (3, rows, zs, RB)

    rotor = to_block(velocity[..., :RB], blocks0)
    inner, outer, stator, seed, mask = load(rotor_offset, rotor, velocity, adjoint_seed, design_mask)
    inner, outer = swapped(inner, outer, "gz", False)
    rotor, stator, seed, solid, outer, inner = call(
        unpack_layers,
        [block, block, (3, width, zs, NR), (width, zs, NR), ext(group + 6), ext(group + 6)],
        rotor_offset, inner, outer, rotor, stator, seed, mask,
    )
    first_in, first_out = swapped(inner, outer, "theta", True)
    visc, rotor, stator = call(
        forward_first,
        [(width + 2, zs, NR), block, block],
        rotor_offset, first_out, first_in, rotor, stator, solid, spread,
        scratch=[ext(2 * width + 4), (3, width + 4, zs, NR)],
    )

    rotor = to_block(rotor, blocks1)
    outer, inner = call(pack_rows, [ext(group + 4)] * 2, rotor_offset, rotor, stator)
    inner, outer = swapped(inner, outer, "theta", True)
    ending, rotor, stator = call(
        forward_last,
        [(3, width, nz, NR), (3, width + 1, nz, RB), block],
        rotor_offset, outer, inner, rotor, stator, solid, spread, back_weight, seed, first_in, first_out,
        scratch=[ext(2 * width + 4), (3, width + 4, zs, NR), (3, width + 2, zs, NR), (width, zs, NR)],
    )

    rotor = to_block(rotor, back1)
    outer, inner, rotor = call(pack_last_rows, [ext(group + 2)] * 2 + [block], rotor_offset, rotor, stator)
    inner, outer = swapped(inner, outer, "theta", True)
    rotor, stator = call(
        adjoint_first,
        [(3, width, nz, RB)] * 2,
        rotor_offset, outer, inner, rotor, stator, solid, back_weight, visc,
        scratch=[ext(2 * width + 2), (3, width + 2, zs, NR), (3, width + 2, zs, NR), (width, nz, NR)],
    )
    rows = exact(rotor, -rotor_offset[0])
    (adjoint,) = call(join, [(3, width, nz, NR)], rotor_offset, rows, stator)
    return ending, adjoint


def solution(mesh):
    return jax.shard_map(
        body,
        mesh=mesh,
        in_specs=(
            P(None, "theta", "gz", None),
            P(None, "theta", "gz", None),
            P(),
            P("theta", "gz", None),
            P(),
        ),
        out_specs=(P(None, "theta", "gz", None), P(None, "theta", "gz", None)),
        check_vma=False,
    )
```

```python
import jax
import jax.numpy as jnp
from jax import lax
from jax.experimental import pallas as pl
from jax.experimental.pallas import tpu as pltpu
from jax.sharding import PartitionSpec as P

NR = 256
RB = 128
BAND = 8
STEPS = 2
LOWER = RB - BAND // 2
UPPER = RB + BAND // 2
ZH = 4


def is_even(axis):
    return 1 - lax.rem(lax.axis_index(axis), 2)


def left_over(shift, width):
    half = width // 2
    return ((shift + half) & (width - 1)) - half


def call(kernel, outs, offsets, *arrays, scratch=()):
    whole = pl.BlockSpec(memory_space=pltpu.VMEM)
    numbers = [] if offsets is None else [offsets]
    return pl.pallas_call(
        kernel,
        out_shape=[jax.ShapeDtypeStruct(shape, jnp.float32) for shape in outs],
        in_specs=[pl.BlockSpec(memory_space=pltpu.SMEM)] * len(numbers) + [whole] * len(arrays),
        out_specs=[whole] * len(outs),
        scratch_shapes=[pltpu.VMEM(shape, jnp.float32) for shape in scratch],
        compiler_params=pltpu.CompilerParams(vmem_limit_bytes=24 << 20),
    )(*numbers, *arrays)


def shifted(x, axis, by):
    peers = lax.axis_size(axis)
    return lax.ppermute(x, axis, [(i, (i + by) % peers) for i in range(peers)])


def nearest(shift, width):
    return (shift + width // 2) // width


def to_block(rotor, blocks):
    peers = lax.axis_size("theta")
    moves = [lambda x, b=b: shifted(x, "theta", b) for b in range(peers)]
    return lax.switch(jnp.mod(blocks, peers), moves, rotor)


def exact(rotor, shift):
    peers = lax.axis_size("theta")
    width = rotor.shape[1]
    group = width // 2
    shift = jnp.mod(shift, width * peers)

    def move(total):
        blocks, rest = divmod(total * group, width)

        def run(x):
            here = shifted(x[:, : width - rest], "theta", blocks)
            before = shifted(x[:, width - rest - group + 1 :], "theta", blocks + 1)
            return jnp.concatenate([before, here], axis=1)

        return run

    return lax.switch(shift // group, [move(i) for i in range(peers * width // group)], rotor)


def swapped(inner, outer, axis, wraps):
    peers = lax.axis_size(axis)
    within = [(i, i ^ 1) for i in range(peers)]
    across = [(i, i + 1 if i % 2 else i - 1) for i in range(peers)]
    if wraps:
        outer = lax.ppermute(outer, axis, [(i, j % peers) for i, j in across])
        return lax.ppermute(inner, axis, within), outer
    inner = lax.ppermute(inner, axis, within)
    return inner, lax.ppermute(outer, axis, [(i, j) for i, j in across if 0 <= j < peers])


def pack_layers(rotor, velocity, seed_in, mask_in, inner, outer, stator, seed, mask, done):
    copies = [
        pltpu.make_async_copy(velocity.at[:, :, :, pl.ds(RB, RB)], stator, done.at[0]),
        pltpu.make_async_copy(seed_in, seed, done.at[1]),
        pltpu.make_async_copy(mask_in, mask, done.at[2]),
    ]
    for copy in copies:
        copy.start()
    for copy in copies:
        copy.wait()
    even = is_even("gz") == 1
    nz = rotor.shape[2]
    for c in range(3):
        for row in range(rotor.shape[1]):
            ends = []
            for z0, z1, z2 in ((nz - ZH, nz - 2, nz - 3 + c), (0, 0, c)):
                solid = mask[row, z2 : z2 + 1, :].astype(jnp.float32)
                blank = jnp.zeros((1, RB), jnp.float32)
                left = [rotor[c, row, z0 : z0 + ZH, :], seed[c, row, z1 : z1 + 2, :RB], solid[:, :RB], blank]
                right = [stator[c, row, z0 : z0 + ZH, :], seed[c, row, z1 : z1 + 2, RB:], solid[:, RB:], blank]
                ends.append([jnp.concatenate(left, axis=0), jnp.concatenate(right, axis=0)])
            top, bottom = ends
            for half in range(2):
                lanes = slice(half * RB, half * RB + RB)
                inner[c, row, :, lanes] = jnp.where(even, top[half], bottom[half])
                outer[c, row, :, lanes] = jnp.where(even, bottom[half], top[half])


def send_rows(h, rotor, stator, extra, inner, outer):
    width = rotor.shape[1]
    reach = width // 2 + h
    even = is_even("theta")
    for target, last in ((inner, even), (outer, 1 - even)):
        target[:, :reach] = rotor[:, pl.ds(last * (width - reach), reach)]
        target[:, reach : reach + h] = stator[:, pl.ds(last * (width - h), h)]
        if extra is not None:
            edge = extra[:, pl.ds(last * (width - 1), 1)]
            target[:, reach + h : reach + h + 1] = edge[..., :RB]
            target[:, reach + h + 1 :] = edge[..., RB:]


def unpack_layers(
    inner, outer, rotor, stator, seed, mask,
    rotor_out, stator_out, seed_out, solid_out, rows_out, rows_in,
):
    even = is_even("gz") == 1
    nz = rotor.shape[2]
    none = jnp.zeros((2, NR), jnp.float32)
    blank = jnp.zeros((1, NR), jnp.float32)
    for row in range(rotor.shape[1]):
        solid_above, solid_below = [], []
        for c in range(3):
            one, two = inner[c, row], outer[c, row]
            above, below = jnp.where(even, one, two), jnp.where(even, two, one)
            halo = jnp.concatenate([above[:ZH], below[:ZH]], axis=0)
            rotor_out[c, row, :nz, :] = rotor[c, row]
            rotor_out[c, row, nz:, :] = halo[:, :RB]
            stator_out[c, row, :nz, :] = stator[c, row]
            stator_out[c, row, nz:, :] = halo[:, RB:]
            seed_out[c, row, :nz, :] = seed[c, row]
            seed_out[c, row, nz:, :] = jnp.concatenate(
                [above[ZH : ZH + 2], none, none, below[ZH : ZH + 2]], axis=0
            )
            solid_above.append(above[ZH + 2 : ZH + 3])
            solid_below.append(below[ZH + 2 : ZH + 3])
        solid_out[row, :nz, :] = mask[row].astype(jnp.float32)
        solid_out[row, nz:, :] = jnp.concatenate(solid_above + [blank, blank] + solid_below, axis=0)
    send_rows(2, rotor_out, stator_out, seed_out, rows_in, rows_out)


def pack_rows(rotor, stator, outer, inner):
    send_rows(2, rotor, stator, None, inner, outer)


def pack_last_rows(packed, stator, outer, inner, rotor):
    _, width, layers, _ = rotor.shape
    nz = packed.shape[2]
    none = jnp.zeros((layers - nz - 2, RB), jnp.float32)
    for c in range(3):
        for row in range(width):
            rotor[c, row, :nz, :] = packed[c, row]
            beyond = packed[c, width, 2 * row : 2 * row + 2, :]
            rotor[c, row, nz:, :] = jnp.concatenate([beyond[:1], none, beyond[1:]], axis=0)
    send_rows(1, rotor, stator, None, inner, outer)


def gather(remain, h, inner, outer, rotor, stator, rotors, field):
    width = rotor.shape[1]
    reach = width // 2 + h
    even = is_even("theta")
    rotors[:, reach : reach + width] = rotor[...]
    rotors[:, pl.ds(even * (reach + width), reach)] = inner[:, :reach]
    rotors[:, pl.ds((1 - even) * (reach + width), reach)] = outer[:, :reach]
    field[..., :RB] = rotors[:, pl.ds(reach - h - remain, width + 2 * h)]
    field[:, h : h + width, :, RB:] = stator[...]
    field[:, pl.ds(even * (h + width), h), :, RB:] = inner[:, reach : reach + h]
    field[:, pl.ds((1 - even) * (h + width), h), :, RB:] = outer[:, reach : reach + h]


def multiply(rows, weight):
    flat = rows.astype(jnp.bfloat16).reshape(-1, NR)
    return rows + jnp.dot(flat, weight[...], preferred_element_type=jnp.float32).reshape(rows.shape)


def around(x, row):
    mid = x[row]
    layers = mid.shape[0]
    lane = lax.broadcasted_iota(jnp.int32, mid.shape, 1)
    rp = jnp.where(lane == NR - 1, 0.0, pltpu.roll(mid, NR - 1, 1))
    rm = jnp.where(lane == 0, 0.0, pltpu.roll(mid, 1, 1))
    return mid, x[row + 1], x[row - 1], pltpu.roll(mid, layers - 1, 0), pltpu.roll(mid, 1, 0), rp, rm


def laplace(mid, tp, tm, zp, zm, rp, rm):
    return tp + tm + zp + zm + rp + rm - 6.0 * mid


def viscosity(sides):
    total = 0.0
    for _, tp, tm, zp, zm, rp, rm in sides:
        total = total + (tp - tm) ** 2 + (zp - zm) ** 2 + (rp - rm) ** 2
    return 0.05 + 0.95 * lax.rsqrt(jnp.sqrt(1.0 + total))


def within_ends(layers):
    place = lax.broadcasted_iota(jnp.int32, (layers, NR), 0)
    nz = layers - 2 * ZH
    layer = lax.axis_index("gz") * nz + jnp.where(place >= layers - ZH, place - layers, place)
    return ((layer >= 0) & (layer < lax.axis_size("gz") * nz)).astype(jnp.float32)


def forward_first(offsets, outer, inner, rotor, stator, solid, weight, visc, u_rotor, u_stator, rotors, w):
    gather(left_over(offsets[0], rotor.shape[1]), 2, inner, outer, rotor, stator, rotors, w)
    for c in range(3):
        w[c] = multiply(w[c], weight)
    width, layers = rotor.shape[1:3]
    inside = within_ends(layers)
    for row in range(width + 2):
        sides = [around(w.at[c], row + 1) for c in range(3)]
        mu = viscosity(sides)
        visc[row] = mu
        if 1 <= row <= width:
            damp = 0.5 * solid[row - 1]
            for c in range(3):
                u = inside * (sides[c][0] + 0.1 * mu * laplace(*sides[c]) - damp * sides[c][0])
                u_rotor[c, row - 1] = u[:, :RB]
                u_stator[c, row - 1] = u[:, RB:]


def forward_last(
    offsets, outer, inner, rotor, stator, solid, weight, back_weight, seed, first_in, first_out,
    ending, lam_rotor, lam_stator, rotors, w, scaled, after,
):
    gather(left_over(offsets[1], rotor.shape[1]), 2, inner, outer, rotor, stator, rotors, w)
    for c in range(3):
        w[c] = multiply(w[c], weight)
    width, layers = rotor.shape[1:3]
    nz = layers - 2 * ZH
    even = is_even("theta") == 1
    inside = within_ends(layers)
    for row in range(width + 2):
        sides = [around(w.at[c], row + 1) for c in range(3)]
        mu = viscosity(sides)
        for c in range(3):
            if 1 <= row <= width:
                lam = seed[c, row - 1]
                scaled[c, row] = mu * lam
                mid = sides[c][0]
                u = mid + 0.1 * mu * laplace(*sides[c]) - 0.5 * solid[row - 1] * mid
                ending[c, row - 1] = u[:nz]
            else:
                one, two = (first_out, first_in) if row == 0 else (first_in, first_out)
                for half in range(2):
                    at = one.shape[1] - 2 + half
                    lam = jnp.where(even, one[c, at], two[c, at])
                    lanes = slice(half * RB, half * RB + RB)
                    scaled[c, row, :, lanes] = mu[:, lanes] * lam
    for c in range(3):
        for row in range(width):
            lam = seed[c, row]
            after[row] = lam + 0.1 * laplace(*around(scaled.at[c], row + 1)) - 0.5 * solid[row] * lam
        lam = inside * multiply(after[...], back_weight)
        lam_stator[c] = lam[..., RB:]
        lam_rotor[c, :width] = lam[:, :nz, :RB]
        for row in range(width):
            lam_rotor[c, width, 2 * row : 2 * row + 1, :] = lam[row, nz : nz + 1, :RB]
            lam_rotor[c, width, 2 * row + 1 : 2 * row + 2, :] = lam[row, layers - 1 :, :RB]


def adjoint_first(
    offsets, outer, inner, rotor, stator, solid, back_weight, visc, b_rotor, b_stator, rotors, lam, scaled, after
):
    gather(left_over(-offsets[1], rotor.shape[1]), 1, inner, outer, rotor, stator, rotors, lam)
    width, layers = rotor.shape[1:3]
    nz = layers - 2 * ZH
    for c in range(3):
        scaled[c] = visc[...] * lam[c]
        for row in range(width):
            mid = lam[c, row + 1]
            a = mid + 0.1 * laplace(*around(scaled.at[c], row + 1)) - 0.5 * solid[row] * mid
            after[row] = a[:nz]
        b = multiply(after[...], back_weight)
        b_rotor[c] = b[..., :RB]
        b_stator[c] = b[..., RB:]


def join(offsets, rows, stator, out):
    width = stator.shape[1]
    group = width // 2
    out[..., :RB] = rows[:, pl.ds(group - 1 - (-offsets[0] & (group - 1)), width)]
    out[..., RB:] = stator[...]


def load(rotor, velocity, seed, mask):
    _, width, nz, _ = velocity.shape
    edge = jax.ShapeDtypeStruct((3, width, 2 * ZH, NR), jnp.float32)
    whole = pl.BlockSpec(memory_space=pltpu.VMEM)
    far = pl.BlockSpec(memory_space=pl.ANY)
    return pl.pallas_call(
        pack_layers,
        out_shape=[
            edge,
            edge,
            jax.ShapeDtypeStruct((3, width, nz, RB), jnp.float32),
            jax.ShapeDtypeStruct(seed.shape, jnp.float32),
            jax.ShapeDtypeStruct(mask.shape, jnp.int32),
        ],
        in_specs=[whole, far, far, far],
        out_specs=[whole] * 5,
        scratch_shapes=[pltpu.SemaphoreType.DMA((3,))],
        compiler_params=pltpu.CompilerParams(vmem_limit_bytes=24 << 20),
    )(rotor, velocity, seed, mask)


def body(velocity, adjoint_seed, rotor_offset, design_mask, interface_band_weight):
    _, width, nz, _ = velocity.shape
    zs = nz + 2 * ZH
    spread = jnp.pad(interface_band_weight, ((0, 0), (LOWER, NR - UPPER)))
    back_weight = jnp.pad(interface_band_weight.T, ((LOWER, NR - UPPER), (0, 0)))
    blocks0 = nearest(rotor_offset[0], width)
    blocks1 = nearest(rotor_offset[1], width)
    back1 = nearest(-rotor_offset[1], width)
    group = width // 2
    block = (3, width, zs, RB)

    def ext(rows):
        return (3, rows, zs, RB)

    rotor = to_block(velocity[..., :RB], blocks0)
    inner, outer, stator, seed, mask = load(rotor, velocity, adjoint_seed, design_mask)
    inner, outer = swapped(inner, outer, "gz", False)
    rotor, stator, seed, solid, outer, inner = call(
        unpack_layers,
        [block, block, (3, width, zs, NR), (width, zs, NR), ext(group + 6), ext(group + 6)],
        None, inner, outer, rotor, stator, seed, mask,
    )
    first_in, first_out = swapped(inner, outer, "theta", True)
    visc, rotor, stator = call(
        forward_first,
        [(width + 2, zs, NR), block, block],
        rotor_offset, first_out, first_in, rotor, stator, solid, spread,
        scratch=[ext(2 * width + 4), (3, width + 4, zs, NR)],
    )

    rotor = to_block(rotor, blocks1)
    outer, inner = call(pack_rows, [ext(group + 4)] * 2, None, rotor, stator)
    inner, outer = swapped(inner, outer, "theta", True)
    ending, rotor, stator = call(
        forward_last,
        [(3, width, nz, NR), (3, width + 1, nz, RB), block],
        rotor_offset, outer, inner, rotor, stator, solid, spread, back_weight, seed, first_in, first_out,
        scratch=[ext(2 * width + 4), (3, width + 4, zs, NR), (3, width + 2, zs, NR), (width, zs, NR)],
    )

    rotor = to_block(rotor, back1)
    outer, inner, rotor = call(pack_last_rows, [ext(group + 2)] * 2 + [block], None, rotor, stator)
    inner, outer = swapped(inner, outer, "theta", True)
    rotor, stator = call(
        adjoint_first,
        [(3, width, nz, RB)] * 2,
        rotor_offset, outer, inner, rotor, stator, solid, back_weight, visc,
        scratch=[ext(2 * width + 2), (3, width + 2, zs, NR), (3, width + 2, zs, NR), (width, nz, NR)],
    )
    rows = exact(rotor, -rotor_offset[0])
    (adjoint,) = call(join, [(3, width, nz, NR)], rotor_offset, rows, stator)
    return ending, adjoint


def solution(mesh):
    return jax.shard_map(
        body,
        mesh=mesh,
        in_specs=(
            P(None, "theta", "gz", None),
            P(None, "theta", "gz", None),
            P(),
            P("theta", "gz", None),
            P(),
        ),
        out_specs=(P(None, "theta", "gz", None), P(None, "theta", "gz", None)),
        check_vma=False,
    )
```

```python
import jax
import jax.numpy as jnp
from jax import lax
from jax.experimental import pallas as pl
from jax.experimental.pallas import tpu as pltpu
from jax.sharding import PartitionSpec as P

NR = 256
RB = 128
BAND = 8
STEPS = 2
LOWER = RB - BAND // 2
UPPER = RB + BAND // 2
ZH = 4


def is_even(axis):
    return 1 - lax.rem(lax.axis_index(axis), 2)


def left_over(shift, width):
    half = width // 2
    return ((shift + half) & (width - 1)) - half


def call(kernel, outs, offsets, *arrays, scratch=()):
    whole = pl.BlockSpec(memory_space=pltpu.VMEM)
    numbers = [] if offsets is None else [offsets]
    return pl.pallas_call(
        kernel,
        out_shape=[jax.ShapeDtypeStruct(shape, jnp.float32) for shape in outs],
        in_specs=[pl.BlockSpec(memory_space=pltpu.SMEM)] * len(numbers) + [whole] * len(arrays),
        out_specs=[whole] * len(outs),
        scratch_shapes=[pltpu.VMEM(shape, jnp.float32) for shape in scratch],
        compiler_params=pltpu.CompilerParams(vmem_limit_bytes=24 << 20),
    )(*numbers, *arrays)


def shifted(x, axis, by):
    peers = lax.axis_size(axis)
    return lax.ppermute(x, axis, [(i, (i + by) % peers) for i in range(peers)])


def nearest(shift, width):
    return (shift + width // 2) // width


def to_block(rotor, blocks):
    peers = lax.axis_size("theta")
    moves = [lambda x, b=b: shifted(x, "theta", b) for b in range(peers)]
    return lax.switch(jnp.mod(blocks, peers), moves, rotor)


def exact(rotor, shift):
    peers = lax.axis_size("theta")
    width = rotor.shape[1]
    group = width // 2
    shift = jnp.mod(shift, width * peers)

    def move(total):
        blocks, rest = divmod(total * group, width)

        def run(x):
            here = shifted(x[:, : width - rest], "theta", blocks)
            before = shifted(x[:, width - rest - group + 1 :], "theta", blocks + 1)
            return jnp.concatenate([before, here], axis=1)

        return run

    return lax.switch(shift // group, [move(i) for i in range(peers * width // group)], rotor)


def swapped(inner, outer, axis, wraps):
    peers = lax.axis_size(axis)
    within = [(i, i ^ 1) for i in range(peers)]
    across = [(i, i + 1 if i % 2 else i - 1) for i in range(peers)]
    if wraps:
        outer = lax.ppermute(outer, axis, [(i, j % peers) for i, j in across])
        return lax.ppermute(inner, axis, within), outer
    inner = lax.ppermute(inner, axis, within)
    return inner, lax.ppermute(outer, axis, [(i, j) for i, j in across if 0 <= j < peers])


def pack_layers(rotor, velocity, seed_in, mask_in, inner, outer, stator, seed, mask, done):
    copies = [
        pltpu.make_async_copy(velocity.at[:, :, :, pl.ds(RB, RB)], stator, done.at[0]),
        pltpu.make_async_copy(seed_in, seed, done.at[1]),
        pltpu.make_async_copy(mask_in, mask, done.at[2]),
    ]
    for copy in copies:
        copy.start()
    for copy in copies:
        copy.wait()
    even = is_even("gz") == 1
    nz = rotor.shape[2]
    for c in range(3):
        for row in range(rotor.shape[1]):
            ends = []
            for z0, z1, z2 in ((nz - ZH, nz - 2, nz - 3 + c), (0, 0, c)):
                solid = mask[row, z2 : z2 + 1, :].astype(jnp.float32)
                blank = jnp.zeros((1, RB), jnp.float32)
                left = [rotor[c, row, z0 : z0 + ZH, :], seed[c, row, z1 : z1 + 2, :RB], solid[:, :RB], blank]
                right = [stator[c, row, z0 : z0 + ZH, :], seed[c, row, z1 : z1 + 2, RB:], solid[:, RB:], blank]
                ends.append([jnp.concatenate(left, axis=0), jnp.concatenate(right, axis=0)])
            top, bottom = ends
            for half in range(2):
                lanes = slice(half * RB, half * RB + RB)
                inner[c, row, :, lanes] = jnp.where(even, top[half], bottom[half])
                outer[c, row, :, lanes] = jnp.where(even, bottom[half], top[half])


def send_rows(h, rotor, stator, extra, inner, outer):
    width = rotor.shape[1]
    reach = width // 2 + h
    even = is_even("theta")
    for target, last in ((inner, even), (outer, 1 - even)):
        target[:, :reach] = rotor[:, pl.ds(last * (width - reach), reach)]
        target[:, reach : reach + h] = stator[:, pl.ds(last * (width - h), h)]
        if extra is not None:
            edge = extra[:, pl.ds(last * (width - 1), 1)]
            target[:, reach + h : reach + h + 1] = edge[..., :RB]
            target[:, reach + h + 1 :] = edge[..., RB:]


def unpack_layers(
    inner, outer, rotor, stator, seed, mask,
    rotor_out, stator_out, seed_out, solid_out, rows_out, rows_in,
):
    even = is_even("gz") == 1
    nz = rotor.shape[2]
    none = jnp.zeros((2, NR), jnp.float32)
    blank = jnp.zeros((1, NR), jnp.float32)
    for row in range(rotor.shape[1]):
        solid_above, solid_below = [], []
        for c in range(3):
            one, two = inner[c, row], outer[c, row]
            above, below = jnp.where(even, one, two), jnp.where(even, two, one)
            halo = jnp.concatenate([above[:ZH], below[:ZH]], axis=0)
            rotor_out[c, row, :nz, :] = rotor[c, row]
            rotor_out[c, row, nz:, :] = halo[:, :RB]
            stator_out[c, row, :nz, :] = stator[c, row]
            stator_out[c, row, nz:, :] = halo[:, RB:]
            seed_out[c, row, :nz, :] = seed[c, row]
            seed_out[c, row, nz:, :] = jnp.concatenate(
                [above[ZH : ZH + 2], none, none, below[ZH : ZH + 2]], axis=0
            )
            solid_above.append(above[ZH + 2 : ZH + 3])
            solid_below.append(below[ZH + 2 : ZH + 3])
        solid_out[row, :nz, :] = mask[row].astype(jnp.float32)
        solid_out[row, nz:, :] = jnp.concatenate(solid_above + [blank, blank] + solid_below, axis=0)
    send_rows(2, rotor_out, stator_out, seed_out, rows_in, rows_out)


def pack_rows(packed, stator, outer, inner, rotor):
    width = rotor.shape[1]
    nz = packed.shape[2]
    none = jnp.zeros((2, RB), jnp.float32)
    for c in range(3):
        for row in range(width):
            rotor[c, row, :nz, :] = packed[c, row]
            one, two, three = [packed[c, width + more, 2 * row : 2 * row + 2, :] for more in range(3)]
            rotor[c, row, nz:, :] = jnp.concatenate([one, two[:1], none, two[1:], three], axis=0)
    send_rows(2, rotor, stator, None, inner, outer)


def pack_last_rows(packed, stator, outer, inner, rotor):
    _, width, layers, _ = rotor.shape
    nz = packed.shape[2]
    none = jnp.zeros((layers - nz - 2, RB), jnp.float32)
    for c in range(3):
        for row in range(width):
            rotor[c, row, :nz, :] = packed[c, row]
            beyond = packed[c, width, 2 * row : 2 * row + 2, :]
            rotor[c, row, nz:, :] = jnp.concatenate([beyond[:1], none, beyond[1:]], axis=0)
    send_rows(1, rotor, stator, None, inner, outer)


def gather(remain, h, inner, outer, rotor, stator, rotors, field):
    width = rotor.shape[1]
    reach = width // 2 + h
    even = is_even("theta")
    rotors[:, reach : reach + width] = rotor[...]
    rotors[:, pl.ds(even * (reach + width), reach)] = inner[:, :reach]
    rotors[:, pl.ds((1 - even) * (reach + width), reach)] = outer[:, :reach]
    field[..., :RB] = rotors[:, pl.ds(reach - h - remain, width + 2 * h)]
    field[:, h : h + width, :, RB:] = stator[...]
    field[:, pl.ds(even * (h + width), h), :, RB:] = inner[:, reach : reach + h]
    field[:, pl.ds((1 - even) * (h + width), h), :, RB:] = outer[:, reach : reach + h]


def multiply(rows, weight):
    flat = rows.astype(jnp.bfloat16).reshape(-1, NR)
    return rows + jnp.dot(flat, weight[...], preferred_element_type=jnp.float32).reshape(rows.shape)


def around(x, row):
    mid = x[row]
    layers = mid.shape[0]
    lane = lax.broadcasted_iota(jnp.int32, mid.shape, 1)
    rp = jnp.where(lane == NR - 1, 0.0, pltpu.roll(mid, NR - 1, 1))
    rm = jnp.where(lane == 0, 0.0, pltpu.roll(mid, 1, 1))
    return mid, x[row + 1], x[row - 1], pltpu.roll(mid, layers - 1, 0), pltpu.roll(mid, 1, 0), rp, rm


def laplace(mid, tp, tm, zp, zm, rp, rm):
    return tp + tm + zp + zm + rp + rm - 6.0 * mid


def viscosity(sides):
    total = 0.0
    for _, tp, tm, zp, zm, rp, rm in sides:
        total = total + (tp - tm) ** 2 + (zp - zm) ** 2 + (rp - rm) ** 2
    return 0.05 + 0.95 * lax.rsqrt(jnp.sqrt(1.0 + total))


def within_ends(layers):
    place = lax.broadcasted_iota(jnp.int32, (layers, NR), 0)
    nz = layers - 2 * ZH
    layer = lax.axis_index("gz") * nz + jnp.where(place >= layers - ZH, place - layers, place)
    return ((layer >= 0) & (layer < lax.axis_size("gz") * nz)).astype(jnp.float32)


def forward_first(offsets, outer, inner, rotor, stator, solid, weight, visc, u_rotor, u_stator, rotors, w):
    gather(left_over(offsets[0], rotor.shape[1]), 2, inner, outer, rotor, stator, rotors, w)
    for c in range(3):
        w[c] = multiply(w[c], weight)
    width, layers = rotor.shape[1:3]
    nz = layers - 2 * ZH
    inside = within_ends(layers)
    for row in range(width + 2):
        sides = [around(w.at[c], row + 1) for c in range(3)]
        mu = viscosity(sides)
        visc[row] = mu
        if 1 <= row <= width:
            damp = 0.5 * solid[row - 1]
            for c in range(3):
                u = inside * (sides[c][0] + 0.1 * mu * laplace(*sides[c]) - damp * sides[c][0])
                u_stator[c, row - 1] = u[:, RB:]
                u_rotor[c, row - 1] = u[:nz, :RB]
                at = 2 * row - 2
                beyond = ((nz, nz + 1), (nz + 2, layers - 3), (layers - 2, layers - 1))
                for more, pair in enumerate(beyond):
                    for one, z in enumerate(pair):
                        u_rotor[c, width + more, at + one : at + one + 1, :] = u[z : z + 1, :RB]


def forward_last(
    offsets, outer, inner, rotor, stator, solid, weight, back_weight, seed, first_in, first_out,
    ending, lam_rotor, lam_stator, rotors, w, scaled, after,
):
    gather(left_over(offsets[1], rotor.shape[1]), 2, inner, outer, rotor, stator, rotors, w)
    for c in range(3):
        w[c] = multiply(w[c], weight)
    width, layers = rotor.shape[1:3]
    nz = layers - 2 * ZH
    even = is_even("theta") == 1
    inside = within_ends(layers)
    for row in range(width + 2):
        sides = [around(w.at[c], row + 1) for c in range(3)]
        mu = viscosity(sides)
        for c in range(3):
            if 1 <= row <= width:
                lam = seed[c, row - 1]
                scaled[c, row] = mu * lam
                mid = sides[c][0]
                u = mid + 0.1 * mu * laplace(*sides[c]) - 0.5 * solid[row - 1] * mid
                ending[c, row - 1] = u[:nz]
            else:
                one, two = (first_out, first_in) if row == 0 else (first_in, first_out)
                for half in range(2):
                    at = one.shape[1] - 2 + half
                    lam = jnp.where(even, one[c, at], two[c, at])
                    lanes = slice(half * RB, half * RB + RB)
                    scaled[c, row, :, lanes] = mu[:, lanes] * lam
    for c in range(3):
        for row in range(width):
            lam = seed[c, row]
            after[row] = lam + 0.1 * laplace(*around(scaled.at[c], row + 1)) - 0.5 * solid[row] * lam
        lam = inside * multiply(after[...], back_weight)
        lam_stator[c] = lam[..., RB:]
        lam_rotor[c, :width] = lam[:, :nz, :RB]
        for row in range(width):
            lam_rotor[c, width, 2 * row : 2 * row + 1, :] = lam[row, nz : nz + 1, :RB]
            lam_rotor[c, width, 2 * row + 1 : 2 * row + 2, :] = lam[row, layers - 1 :, :RB]


def adjoint_first(
    offsets, outer, inner, rotor, stator, solid, back_weight, visc, b_rotor, b_stator, rotors, lam, scaled, after
):
    gather(left_over(-offsets[1], rotor.shape[1]), 1, inner, outer, rotor, stator, rotors, lam)
    width, layers = rotor.shape[1:3]
    nz = layers - 2 * ZH
    for c in range(3):
        scaled[c] = visc[...] * lam[c]
        for row in range(width):
            mid = lam[c, row + 1]
            a = mid + 0.1 * laplace(*around(scaled.at[c], row + 1)) - 0.5 * solid[row] * mid
            after[row] = a[:nz]
        b = multiply(after[...], back_weight)
        b_rotor[c] = b[..., :RB]
        b_stator[c] = b[..., RB:]


def join(offsets, rows, stator, out):
    width = stator.shape[1]
    group = width // 2
    out[..., :RB] = rows[:, pl.ds(group - 1 - (-offsets[0] & (group - 1)), width)]
    out[..., RB:] = stator[...]


def load(rotor, velocity, seed, mask):
    _, width, nz, _ = velocity.shape
    edge = jax.ShapeDtypeStruct((3, width, 2 * ZH, NR), jnp.float32)
    whole = pl.BlockSpec(memory_space=pltpu.VMEM)
    far = pl.BlockSpec(memory_space=pl.ANY)
    return pl.pallas_call(
        pack_layers,
        out_shape=[
            edge,
            edge,
            jax.ShapeDtypeStruct((3, width, nz, RB), jnp.float32),
            jax.ShapeDtypeStruct(seed.shape, jnp.float32),
            jax.ShapeDtypeStruct(mask.shape, jnp.int32),
        ],
        in_specs=[whole, far, far, far],
        out_specs=[whole] * 5,
        scratch_shapes=[pltpu.SemaphoreType.DMA((3,))],
        compiler_params=pltpu.CompilerParams(vmem_limit_bytes=24 << 20),
    )(rotor, velocity, seed, mask)


def body(velocity, adjoint_seed, rotor_offset, design_mask, interface_band_weight):
    _, width, nz, _ = velocity.shape
    zs = nz + 2 * ZH
    spread = jnp.pad(interface_band_weight, ((0, 0), (LOWER, NR - UPPER)))
    back_weight = jnp.pad(interface_band_weight.T, ((LOWER, NR - UPPER), (0, 0)))
    blocks0 = nearest(rotor_offset[0], width)
    blocks1 = nearest(rotor_offset[1], width)
    back1 = nearest(-rotor_offset[1], width)
    group = width // 2
    block = (3, width, zs, RB)

    def ext(rows):
        return (3, rows, zs, RB)

    rotor = to_block(velocity[..., :RB], blocks0)
    inner, outer, stator, seed, mask = load(rotor, velocity, adjoint_seed, design_mask)
    inner, outer = swapped(inner, outer, "gz", False)
    rotor, stator, seed, solid, outer, inner = call(
        unpack_layers,
        [block, block, (3, width, zs, NR), (width, zs, NR), ext(group + 6), ext(group + 6)],
        None, inner, outer, rotor, stator, seed, mask,
    )
    first_in, first_out = swapped(inner, outer, "theta", True)
    visc, rotor, stator = call(
        forward_first,
        [(width + 2, zs, NR), (3, width + 3, nz, RB), block],
        rotor_offset, first_out, first_in, rotor, stator, solid, spread,
        scratch=[ext(2 * width + 4), (3, width + 4, zs, NR)],
    )

    rotor = to_block(rotor, blocks1)
    outer, inner, rotor = call(pack_rows, [ext(group + 4)] * 2 + [block], None, rotor, stator)
    inner, outer = swapped(inner, outer, "theta", True)
    ending, rotor, stator = call(
        forward_last,
        [(3, width, nz, NR), (3, width + 1, nz, RB), block],
        rotor_offset, outer, inner, rotor, stator, solid, spread, back_weight, seed, first_in, first_out,
        scratch=[ext(2 * width + 4), (3, width + 4, zs, NR), (3, width + 2, zs, NR), (width, zs, NR)],
    )

    rotor = to_block(rotor, back1)
    outer, inner, rotor = call(pack_last_rows, [ext(group + 2)] * 2 + [block], None, rotor, stator)
    inner, outer = swapped(inner, outer, "theta", True)
    rotor, stator = call(
        adjoint_first,
        [(3, width, nz, RB)] * 2,
        rotor_offset, outer, inner, rotor, stator, solid, back_weight, visc,
        scratch=[ext(2 * width + 2), (3, width + 2, zs, NR), (3, width + 2, zs, NR), (width, nz, NR)],
    )
    rows = exact(rotor, -rotor_offset[0])
    (adjoint,) = call(join, [(3, width, nz, NR)], rotor_offset, rows, stator)
    return ending, adjoint


def solution(mesh):
    return jax.shard_map(
        body,
        mesh=mesh,
        in_specs=(
            P(None, "theta", "gz", None),
            P(None, "theta", "gz", None),
            P(),
            P("theta", "gz", None),
            P(),
        ),
        out_specs=(P(None, "theta", "gz", None), P(None, "theta", "gz", None)),
        check_vma=False,
    )
```
